32 devices in a mesh: energy: 8 (over z, y), momentum: 4 (over x, core).
Axes of the slice: x: 2, y: 2, z: 4, core: 2. Of those that a mesh axis runs over, the one named last changes fastest.
Arguments:
- lesser: bfloat16 [8, 4, 2, 512, 512], P('energy', 'momentum'), may hold values from -6 to 6
- greater: bfloat16 [8, 4, 2, 512, 512], P('energy', 'momentum'), may hold values from -6 to 6
- retarded: bfloat16 [8, 4, 2, 512, 512], P('energy', 'momentum'), may hold values from -4.1875 to 4.1875
- occupation: float32 [2], replicated, may hold values from 0.1 to 2
- shift_slots: int32 [2, 2, 8], replicated, may hold values from 0 to 8, as said below
- coupling: int32 [2, 4, 4], replicated, may hold values from 1 to 8
Outputs:
- lesser_new: bfloat16 [8, 4, 2, 512, 512], P('energy', 'momentum')
- greater_new: bfloat16 [8, 4, 2, 512, 512], P('energy', 'momentum')
- retarded_new: bfloat16 [8, 4, 2, 512, 512], P('energy', 'momentum')
The draws below stay inside these ranges and needn't reach their ends.
Inputs may be any that keep to these rules, and one draw needn't show every extreme that they name: The energies of the grid are held in slots in an order of their own, one energy a slot. Mode m has one shift, the same for all slots: shift_slots[m, 0, j] is the slot of the energy that lies that shift below the energy of slot j, shift_slots[m, 1, j] the slot of the energy as far above it, and 8 where that energy lies outside the grid.
All inputs are finite; a program needn't handle non-finite values.
Results may differ from the reference program's by a relative error of at most 0.0064.
Values may be sent and summed in bfloat16 or wider, within the bound.
A program may use at most 64 MiB of HBM per device.

```python
import math
import jax
import jax.numpy as jnp
from jax import lax

B = 512
MODES = 2
ENERGIES = 8
MOMENTA = 4


def draw_shift_slots(key, part):
    order_key = jax.random.fold_in(key, 11)
    shift_key = jax.random.fold_in(key, 12)
    energy_of = jax.random.permutation(order_key, ENERGIES).astype(jnp.int32)
    slot_of = jnp.zeros((ENERGIES,), jnp.int32).at[energy_of].set(jnp.arange(ENERGIES, dtype=jnp.int32))
    shifts = jax.random.randint(shift_key, (MODES,), 1, ENERGIES // 2 + 1).astype(jnp.int32)
    below = energy_of[None, :] - shifts[:, None]
    above = energy_of[None, :] + shifts[:, None]
    below_slot = jnp.where(below >= 0, slot_of[jnp.clip(below, 0, ENERGIES - 1)], ENERGIES)
    above_slot = jnp.where(above < ENERGIES, slot_of[jnp.clip(above, 0, ENERGIES - 1)], ENERGIES)
    return jnp.stack([below_slot, above_slot], axis=1).astype(jnp.int32)


def touch_ends(entries, rng, least, high):
    extent = entries.shape
    index_at = [jax.random.randint(jax.random.fold_in(rng, axis), (), 0, extent[axis]) for axis in range(len(extent))]
    entries = entries.at[tuple(index_at)].set(least)
    longest = extent.index(max(extent))
    index_at[longest] = (index_at[longest] + 1) % extent[longest]
    return entries.at[tuple(index_at)].set(high)


def steps_of(own_key, shape, cuts, low, top_value):
    loudness, own = 1.0, jax.random.fold_in(own_key, 6)
    for position, parts in cuts:
        heights = jnp.exp(jax.random.uniform(jax.random.fold_in(own, position), (parts,), jnp.float32, low / len(cuts), top_value / len(cuts)))
        loudness = loudness * jnp.repeat(heights, shape[position] // parts).reshape([-1 if axis == position else 1 for axis in range(len(shape))])
    return loudness


def gaussian(key, dims, spread, reach, shards=(), held_as=jnp.bfloat16):
    values = spread * jax.random.normal(key, dims, jnp.float32)
    if shards:
        values = values * steps_of(key, dims, shards, -0.22, 0.18)
    return jnp.clip(values, -reach, reach).astype(held_as)


def setup_inputs(seed: int = 0) -> dict:
    key_list = jax.random.split(jax.random.key(seed), 7)
    return {
        "lesser": gaussian(key_list[0], (ENERGIES, MOMENTA, 2, B, B), 1.0, 6.0, ((0, 8), (1, 4))),
        "greater": gaussian(key_list[1], (ENERGIES, MOMENTA, 2, B, B), 1.0, 6.0, ((0, 8), (1, 4))),
        "retarded": gaussian(key_list[2], (ENERGIES, MOMENTA, 2, B, B), 0.7, 4.1875, ((0, 8), (1, 4))),
        "occupation": jnp.clip(jnp.exp(jax.random.uniform(key_list[3], (MODES,), jnp.float32, math.log(0.1), math.log(2.0))), 0.1, 2.0),
        "shift_slots": draw_shift_slots(jax.random.fold_in(key_list[6], 71), 0),
        "coupling": touch_ends(jax.random.randint(key_list[5], (MODES, MOMENTA, MOMENTA), 1, 9), jax.random.fold_in(key_list[5], 1), 1, 8).astype(jnp.int32),
    }


def matrix_product(former, latter):
    return jnp.matmul(former.astype(jnp.float32), latter.astype(jnp.float32), precision=lax.Precision.HIGHEST)


def complex_product(former, latter):
    former_re = former[..., 0, :, :]
    former_im = former[..., 1, :, :]
    latter_re = latter[..., 0, :, :]
    latter_im = latter[..., 1, :, :]
    real_part = matrix_product(former_re, latter_re) - matrix_product(former_im, latter_im)
    imag_part = matrix_product(former_re, latter_im) + matrix_product(former_im, latter_re)
    return jnp.stack([real_part, imag_part], axis=-3)


def adjoint_product(former, propagator):
    former_re = former[..., 0, :, :]
    former_im = former[..., 1, :, :]
    prop_re = jnp.swapaxes(propagator[..., 0, :, :], -1, -2)
    prop_im = jnp.swapaxes(propagator[..., 1, :, :], -1, -2)
    real_part = matrix_product(former_re, prop_re) + matrix_product(former_im, prop_im)
    imag_part = matrix_product(former_im, prop_re) - matrix_product(former_re, prop_im)
    return jnp.stack([real_part, imag_part], axis=-3)


def reference(lesser, greater, retarded, occupation, shift_slots, coupling):
    factor = 1.0 / (B * 4.0 * (MODES * MOMENTA) ** 0.5)
    filler = jnp.zeros((1, MOMENTA, 2, B, B), jnp.bfloat16)
    padded_less = jnp.concatenate([lesser, filler], axis=0)
    padded_more = jnp.concatenate([greater, filler], axis=0)
    weights = coupling.astype(jnp.float32)

    def one_slot(inputs):
        target, propagator = inputs
        total_less = jnp.zeros((MOMENTA, 2, B, B), jnp.float32)
        total_more = jnp.zeros((MOMENTA, 2, B, B), jnp.float32)
        for branch in range(MODES):
            phonons = occupation[branch]
            below_less = padded_less[shift_slots[branch, 0, target]].astype(jnp.float32)
            above_less = padded_less[shift_slots[branch, 1, target]].astype(jnp.float32)
            below_more = padded_more[shift_slots[branch, 0, target]].astype(jnp.float32)
            above_more = padded_more[shift_slots[branch, 1, target]].astype(jnp.float32)
            mix_less = phonons * below_less + (phonons + 1.0) * above_less
            mix_more = (phonons + 1.0) * below_more + phonons * above_more
            total_less = total_less + jnp.einsum("kq,qxab->kxab", weights[branch], mix_less, precision=lax.Precision.HIGHEST)
            total_more = total_more + jnp.einsum("kq,qxab->kxab", weights[branch], mix_more, precision=lax.Precision.HIGHEST)
        sigma_less = (total_less * factor).astype(jnp.bfloat16)
        sigma_more = (total_more * factor).astype(jnp.bfloat16)
        sigma_ret = ((sigma_more.astype(jnp.float32) - sigma_less.astype(jnp.float32)) * 0.5).astype(jnp.bfloat16)
        stacked = jnp.stack([sigma_less, sigma_more, sigma_ret])
        halfway = complex_product(propagator[None], stacked).astype(jnp.bfloat16)
        less_new = adjoint_product(halfway[0], propagator).astype(jnp.bfloat16)
        more_new = adjoint_product(halfway[1], propagator).astype(jnp.bfloat16)
        ret_new = (propagator.astype(jnp.float32) + complex_product(halfway[2], propagator)).astype(jnp.bfloat16)
        return less_new, more_new, ret_new

    targets = jnp.arange(ENERGIES, dtype=jnp.int32)
    lesser_new, greater_new, retarded_new = lax.map(one_slot, (targets, retarded))
    return (lesser_new, greater_new, retarded_new)
```

```python
import functools

import jax
import jax.numpy as jnp
from jax import lax
from jax.experimental import pallas as pl
from jax.experimental.pallas import tpu as pltpu
from jax.sharding import PartitionSpec as P

MESH = pl.DeviceIdType.MESH


def dot(a, b):
    return jnp.dot(a, b, preferred_element_type=jnp.float32)


def dot_t(a, b):
    return lax.dot_general(a, b, (((1,), (1,)), ((), ())), preferred_element_type=jnp.float32)


def kernel(
    sizes,
    factor,
    less_ref,
    more_ref,
    ret_ref,
    occ_ref,
    shift_ref,
    coup_ref,
    less_out,
    more_out,
    ret_out,
    recv_less,
    recv_more,
    mixed,
    send_less,
    send_more,
    sig_less,
    sig_more,
    half,
    send_sem,
    recv_sem,
    own_sem,
):
    energies, momenta, modes, parts, rows, cols, row_groups, col_groups = sizes
    n = energies * momenta
    my_e, my_m = lax.axis_index("energy"), lax.axis_index("momentum")
    me = my_e * momenta + my_m
    order = row_groups * rows

    def partner(i):
        t = i // momenta
        up = energies // 2 + t // 2
        down = energies // 2 - (t + 1) // 2
        offset = up + (t % 2) * (down - up)
        e = lax.rem(my_e + offset, energies)
        m = lax.rem(my_m + i % momenta + 1, momenta)
        return e, m

    def piece(ref, lead, d):
        row = pl.multiple_of(lax.rem(d, row_groups) * rows, rows)
        rest = d // row_groups
        col = pl.multiple_of(lax.rem(rest, col_groups) * cols, cols)
        part = (rest // col_groups) * parts
        index = (pl.ds(part, parts), pl.ds(row, rows), pl.ds(col, cols))
        return ref.at[(0,) * lead + index]

    barrier = pltpu.get_barrier_semaphore()

    def greet(i, carry):
        pl.semaphore_signal(barrier, inc=1, device_id=partner(i), device_id_type=MESH)
        return carry

    lax.fori_loop(0, n - 1, greet, 0)
    own_less = pltpu.make_async_copy(piece(less_ref, 2, me), recv_less.at[me], own_sem.at[0])
    own_more = pltpu.make_async_copy(piece(more_ref, 2, me), recv_more.at[me], own_sem.at[1])
    own_less.start()
    own_more.start()
    pl.semaphore_wait(barrier, n - 1)

    def forward(ref, landing, which):
        def send(i, carry):
            e, m = partner(i)
            pltpu.make_async_remote_copy(
                src_ref=piece(ref, 2, e * momenta + m),
                dst_ref=landing.at[me],
                send_sem=send_sem.at[which],
                recv_sem=recv_sem.at[which],
                device_id=(e, m),
                device_id_type=MESH,
            ).start()
            return carry

        lax.fori_loop(0, n - 1, send, 0)

    def back(ref, landing, which):
        def send(i, carry):
            e, m = partner(i)
            pltpu.make_async_remote_copy(
                src_ref=ref.at[e * momenta + m],
                dst_ref=piece(landing, 0, me),
                send_sem=send_sem.at[which],
                recv_sem=recv_sem.at[which],
                device_id=(e, m),
                device_id_type=MESH,
            ).start()
            return carry

        lax.fori_loop(0, n - 1, send, 0)

    def wait_all(sem):
        span = recv_less.at[pl.ds(0, n - 1)]
        pltpu.make_async_copy(span, span, sem).wait()

    forward(less_ref, recv_less, 0)
    forward(more_ref, recv_more, 1)

    mixed[:, energies] = jnp.zeros((modes, momenta, parts, rows, cols), jnp.float32)
    width = min(cols, 256)
    blocks = parts * (cols // width)

    def mix(recv, send, add_below, add_above):
        def over_momenta(i, carry):
            s, b = i // blocks, i % blocks
            part = b // (cols // width)
            at = pl.ds(pl.multiple_of((b % (cols // width)) * width, width), width)
            terms = [recv[s * momenta + q, part, :, at].astype(jnp.float32) for q in range(momenta)]
            for m in range(modes):
                for k in range(momenta):
                    total = coup_ref[m, k, 0].astype(jnp.float32) * terms[0]
                    for q in range(1, momenta):
                        total += coup_ref[m, k, q].astype(jnp.float32) * terms[q]
                    mixed[m, s, k, part, :, at] = total
            return carry

        lax.fori_loop(0, energies * blocks, over_momenta, 0)

        def over_energies(i, carry):
            j, b = i // blocks, i % blocks
            part = b // (cols // width)
            at = pl.ds(pl.multiple_of((b % (cols // width)) * width, width), width)
            for k in range(momenta):
                total = None
                for m in range(modes):
                    phonons = occ_ref[m]
                    for side, add in ((0, add_below), (1, add_above)):
                        term = ((phonons + add) * factor) * mixed[m, shift_ref[m, side, j], k, part, :, at]
                        total = term if total is None else total + term
                send[j * momenta + k, part, :, at] = total.astype(jnp.bfloat16)
            return carry

        lax.fori_loop(0, energies * blocks, over_energies, 0)

    tile = min(order, 256)

    def halfway(sigma_of):
        def step(i, carry):
            at = pl.ds(pl.multiple_of(i * tile, tile), tile)
            re, im = sigma_of(0, at), sigma_of(1, at)
            ret_re, ret_im = ret_ref[0, 0, 0], ret_ref[0, 0, 1]
            half[0, :, at] = (dot(ret_re, re) - dot(ret_im, im)).astype(jnp.bfloat16)
            half[1, :, at] = (dot(ret_re, im) + dot(ret_im, re)).astype(jnp.bfloat16)
            return carry

        lax.fori_loop(0, order // tile, step, 0)

    def adjoint(out):
        def step(i, carry):
            at = pl.ds(pl.multiple_of(i * tile, tile), tile)
            ret_re, ret_im = ret_ref[0, 0, 0, at], ret_ref[0, 0, 1, at]
            re, im = half[0], half[1]
            out[0, 0, 0, :, at] = (dot_t(re, ret_re) + dot_t(im, ret_im)).astype(jnp.bfloat16)
            out[0, 0, 1, :, at] = (dot_t(im, ret_re) - dot_t(re, ret_im)).astype(jnp.bfloat16)
            return carry

        lax.fori_loop(0, order // tile, step, 0)

    own_less.wait()
    wait_all(recv_sem.at[0])
    mix(recv_less, send_less, 0.0, 1.0)
    back(send_less, sig_less, 2)
    keep_less = pltpu.make_async_copy(send_less.at[me], piece(sig_less, 0, me), own_sem.at[0])
    keep_less.start()

    own_more.wait()
    wait_all(recv_sem.at[1])
    mix(recv_more, send_more, 1.0, 0.0)
    back(send_more, sig_more, 3)
    keep_more = pltpu.make_async_copy(send_more.at[me], piece(sig_more, 0, me), own_sem.at[1])
    keep_more.start()

    keep_less.wait()
    wait_all(recv_sem.at[2])
    halfway(lambda x, at: sig_less[x, :, at])
    adjoint(less_out)

    keep_more.wait()
    wait_all(recv_sem.at[3])
    halfway(lambda x, at: sig_more[x, :, at])
    adjoint(more_out)

    def sigma_ret(x, at):
        more = sig_more[x, :, at].astype(jnp.float32)
        less = sig_less[x, :, at].astype(jnp.float32)
        return ((more - less) * 0.5).astype(jnp.bfloat16)

    halfway(sigma_ret)

    def dyson(i, carry):
        at = pl.ds(pl.multiple_of(i * tile, tile), tile)
        ret_re, ret_im = ret_ref[0, 0, 0, :, at], ret_ref[0, 0, 1, :, at]
        re, im = half[0], half[1]
        ret_out[0, 0, 0, :, at] = (
            ret_re.astype(jnp.float32) + (dot(re, ret_re) - dot(im, ret_im))
        ).astype(jnp.bfloat16)
        ret_out[0, 0, 1, :, at] = (
            ret_im.astype(jnp.float32) + (dot(re, ret_im) + dot(im, ret_re))
        ).astype(jnp.bfloat16)
        return carry

    lax.fori_loop(0, order // tile, dyson, 0)
    for which in range(4):
        wait_all(send_sem.at[which])


def per_device(energies, momenta, lesser, greater, retarded, occupation, shift_slots, coupling):
    n = energies * momenta
    modes = coupling.shape[0]
    order = lesser.shape[-1]
    factor = 1.0 / (order * 4.0 * (modes * momenta) ** 0.5)
    row_groups = min(n, order // 16)
    col_groups = min(n // row_groups, order // 128)
    part_groups = n // (row_groups * col_groups)
    parts, rows, cols = 2 // part_groups, order // row_groups, order // col_groups
    sizes = (energies, momenta, modes, parts, rows, cols, row_groups, col_groups)
    vmem = pl.BlockSpec(memory_space=pltpu.VMEM)
    smem = pl.BlockSpec(memory_space=pltpu.SMEM)
    hbm = pl.BlockSpec(memory_space=pl.ANY)
    exchanged = pltpu.VMEM((n, parts, rows, cols), jnp.bfloat16)
    block = pltpu.VMEM((2, order, order), jnp.bfloat16)
    return pl.pallas_call(
        functools.partial(kernel, sizes, factor),
        out_shape=tuple(jax.ShapeDtypeStruct(lesser.shape, jnp.bfloat16) for _ in range(3)),
        in_specs=[hbm, hbm, vmem, smem, smem, smem],
        out_specs=(vmem, vmem, vmem),
        scratch_shapes=[
            exchanged,
            exchanged,
            pltpu.VMEM((modes, energies + 1, momenta, parts, rows, cols), jnp.float32),
            exchanged,
            exchanged,
            block,
            block,
            block,
            pltpu.SemaphoreType.DMA((4,)),
            pltpu.SemaphoreType.DMA((4,)),
            pltpu.SemaphoreType.DMA((2,)),
        ],
        compiler_params=pltpu.CompilerParams(
            collective_id=0, has_side_effects=True, vmem_limit_bytes=40 * 1024 * 1024
        ),
        cost_estimate=pl.CostEstimate(
            flops=48 * order**3, bytes_accessed=24 * order * order, transcendentals=0
        ),
    )(lesser, greater, retarded, occupation, shift_slots, coupling)


def solution(mesh):
    split = P("energy", "momentum", None, None, None)
    return jax.shard_map(
        functools.partial(per_device, mesh.shape["energy"], mesh.shape["momentum"]),
        mesh=mesh,
        in_specs=(split, split, split, P(), P(), P()),
        out_specs=(split, split, split),
        check_vma=False,
    )
```

```python
import functools

import jax
import jax.numpy as jnp
from jax import lax
from jax.experimental import pallas as pl
from jax.experimental.pallas import tpu as pltpu
from jax.sharding import PartitionSpec as P

MESH = pl.DeviceIdType.MESH


def dot(a, b):
    return jnp.dot(a, b, preferred_element_type=jnp.float32)


def dot_t(a, b):
    return lax.dot_general(a, b, (((1,), (1,)), ((), ())), preferred_element_type=jnp.float32)


def kernel(
    sizes,
    factor,
    less_ref,
    more_ref,
    ret_ref,
    occ_ref,
    shift_ref,
    coup_ref,
    less_out,
    more_out,
    ret_out,
    ret_held,
    occ_held,
    shift_held,
    coup_held,
    recv_less,
    recv_more,
    mixed,
    send_less,
    send_more,
    sig_less,
    sig_more,
    half,
    half_ret,
    half_less,
    sum_more,
    sum_ret,
    send_sem,
    recv_sem,
    own_sem,
    load_sem,
):
    energies, momenta, modes, parts, rows, cols, row_groups, col_groups = sizes
    n = energies * momenta
    my_e, my_m = lax.axis_index("energy"), lax.axis_index("momentum")
    me = my_e * momenta + my_m
    order = row_groups * rows

    pieces = max(cols // 256, 1)
    width = cols // pieces

    my_row = [lax.rem(my_m + m + 1, momenta) for m in range(momenta)]

    def others(act):
        def at_energy(t, carry):
            odd = lax.rem(t, 2)
            half_t = lax.div(t + odd, 2)
            offset = energies // 2 + half_t - 2 * odd * half_t
            e = lax.rem(my_e + offset, energies)
            for m in my_row:
                act(e, m)
            return carry

        lax.fori_loop(0, energies - 1, at_energy, 0)
        for m in my_row[:-1]:
            act(my_e, m)

    def piece(ref, lead, d, begin, count):
        row = pl.multiple_of(lax.rem(d, row_groups) * rows, rows)
        rest = lax.div(d, row_groups)
        col = pl.multiple_of(lax.rem(rest, col_groups) * cols, cols) + begin
        part = lax.div(rest, col_groups) * parts
        index = (pl.ds(part, parts), pl.ds(row, rows), pl.ds(col, count))
        return ref.at[(0,) * lead + index]

    barrier = pltpu.get_barrier_semaphore()

    def greet(e, m):
        pl.semaphore_signal(barrier, inc=1, device_id=(e, m), device_id_type=MESH)

    others(greet)
    loads = [
        pltpu.make_async_copy(piece(less_ref, 2, me, 0, cols), recv_less.at[me], own_sem.at[0]),
        pltpu.make_async_copy(piece(more_ref, 2, me, 0, cols), recv_more.at[me], own_sem.at[1]),
        pltpu.make_async_copy(ret_ref, ret_held, load_sem.at[0]),
        pltpu.make_async_copy(occ_ref, occ_held, load_sem.at[1]),
        pltpu.make_async_copy(shift_ref, shift_held, load_sem.at[2]),
        pltpu.make_async_copy(coup_ref, coup_held, load_sem.at[3]),
    ]
    for load in loads:
        load.start()
    pl.semaphore_wait(barrier, n - 1)

    def forward(ref, landing, which):
        def send(e, m):
            pltpu.make_async_remote_copy(
                src_ref=piece(ref, 2, e * momenta + m, 0, cols),
                dst_ref=landing.at[me],
                send_sem=send_sem.at[which],
                recv_sem=recv_sem.at[which],
                device_id=(e, m),
                device_id_type=MESH,
            ).start()

        others(send)

    def back(ref, landing, begin, count, which):
        def send(e, m):
            pltpu.make_async_remote_copy(
                src_ref=ref.at[e * momenta + m, :, :, pl.ds(begin, count)],
                dst_ref=piece(landing, 0, me, begin, count),
                send_sem=send_sem.at[which],
                recv_sem=recv_sem.at[which],
                device_id=(e, m),
                device_id_type=MESH,
            ).start()

        others(send)

    def wait_all(sem, count):
        span = recv_less.at[pl.ds(0, n - 1), :, :, pl.ds(0, count)]
        pltpu.make_async_copy(span, span, sem).wait()

    forward(less_ref, recv_less, 0)
    forward(more_ref, recv_more, 1)

    mixed[:, energies] = jnp.zeros((modes, momenta, parts, rows, cols), jnp.float32)

    def mix(recv, send, add_below, add_above, begin, count):
        step = min(count, 256)
        blocks = parts * (count // step)

        def place(i):
            b = lax.rem(i, blocks)
            col = begin + lax.rem(b, count // step) * step
            at = pl.ds(pl.multiple_of(col, step), step)
            return lax.div(i, blocks), lax.div(b, count // step), at

        def over_momenta(i, carry):
            s, part, at = place(i)
            terms = [recv[s * momenta + q, part, :, at].astype(jnp.float32) for q in range(momenta)]
            for m in range(modes):
                for k in range(momenta):
                    total = coup_held[m, k, 0].astype(jnp.float32) * terms[0]
                    for q in range(1, momenta):
                        total += coup_held[m, k, q].astype(jnp.float32) * terms[q]
                    mixed[m, s, k, part, :, at] = total
            return carry

        lax.fori_loop(0, energies * blocks, over_momenta, 0)

        def over_energies(i, carry):
            j, part, at = place(i)
            for k in range(momenta):
                total = None
                for m in range(modes):
                    phonons = occ_held[m]
                    for side, add in ((0, add_below), (1, add_above)):
                        term = ((phonons + add) * factor) * mixed[m, shift_held[m, side, j], k, part, :, at]
                        total = term if total is None else total + term
                send[j * momenta + k, part, :, at] = total.astype(jnp.bfloat16)
            return carry

        lax.fori_loop(0, energies * blocks, over_energies, 0)

    for load in loads[2:]:
        load.wait()
    loads[0].wait()
    wait_all(recv_sem.at[0], cols)
    mix(recv_less, send_less, 0.0, 1.0, 0, cols)
    back(send_less, sig_less, 0, cols, 2)
    keep_less = pltpu.make_async_copy(send_less.at[me], piece(sig_less, 0, me, 0, cols), own_sem.at[0])
    keep_less.start()

    loads[1].wait()
    wait_all(recv_sem.at[1], cols)
    keeps = []
    for c in range(pieces):
        begin = c * width
        mix(recv_more, send_more, 1.0, 0.0, begin, width)
        back(send_more, sig_more, begin, width, 3 + c)
        keep = pltpu.make_async_copy(
            send_more.at[me, :, :, pl.ds(begin, width)],
            piece(sig_more, 0, me, begin, width),
            own_sem.at[1 + c],
        )
        keep.start()
        keeps.append(keep)

    ret_re, ret_im = ret_held.at[0, 0, 0], ret_held.at[0, 0, 1]

    def halfway(sigma, at):
        re, im = sigma[0, :, at], sigma[1, :, at]
        left_re, left_im = ret_re[...], ret_im[...]
        return (
            dot(left_re, re) - dot(left_im, im),
            dot(left_re, im) + dot(left_im, re),
        )

    def adjoint(which, at, to):
        re, im = half[0, :, at], half[1, :, at]
        right_re, right_im = ret_re[to, at], ret_im[to, at]
        if which == 0:
            return dot_t(re, right_re) + dot_t(im, right_im)
        return dot_t(im, right_re) - dot_t(re, right_im)

    def dyson(which, at, to):
        re, im = half_ret[0, :, at], half_ret[1, :, at]
        right_re, right_im = ret_re[at, to], ret_im[at, to]
        if which == 0:
            return dot(re, right_re) - dot(im, right_im)
        return dot(re, right_im) + dot(im, right_re)

    tile = min(order, 256)
    tiles = [pl.ds(t * tile, tile) for t in range(order // tile)]

    keep_less.wait()
    wait_all(recv_sem.at[2], cols)
    for at in tiles:
        re, im = halfway(sig_less, at)
        half_less[0, :, at] = re
        half_less[1, :, at] = im
        half[0, :, at] = re.astype(jnp.bfloat16)
        half[1, :, at] = im.astype(jnp.bfloat16)
    for to in tiles:
        for x in range(2):
            less_out[0, 0, x, :, to] = adjoint(x, pl.ds(0, order), to).astype(jnp.bfloat16)

    stages = pieces if col_groups == 1 else 1
    span = order // stages
    for c in range(pieces):
        keeps[c].wait()
        wait_all(recv_sem.at[3 + c], width)
        if stages == 1 and c < pieces - 1:
            continue
        stage = c if stages > 1 else 0
        last = stage == stages - 1
        for t in range(span // tile):
            at = pl.ds(stage * span + t * tile, tile)
            for x, value in enumerate(halfway(sig_more, at)):
                half[x, :, at] = value.astype(jnp.bfloat16)
                half_ret[x, :, at] = ((value - half_less[x, :, at]) * 0.5).astype(jnp.bfloat16)
        at = pl.ds(stage * span, span)
        for to in tiles:
            for x in range(2):
                more, ret = adjoint(x, at, to), dyson(x, at, to)
                if stage > 0:
                    more += sum_more[x, :, to]
                    ret += sum_ret[x, :, to]
                if last:
                    more_out[0, 0, x, :, to] = more.astype(jnp.bfloat16)
                    ret += (ret_re, ret_im)[x][:, to].astype(jnp.float32)
                    ret_out[0, 0, x, :, to] = ret.astype(jnp.bfloat16)
                else:
                    sum_more[x, :, to] = more
                    sum_ret[x, :, to] = ret
    for which in range(3):
        wait_all(send_sem.at[which], cols)
    for c in range(pieces):
        wait_all(send_sem.at[3 + c], width)


def per_device(energies, momenta, lesser, greater, retarded, occupation, shift_slots, coupling):
    n = energies * momenta
    modes = coupling.shape[0]
    order = lesser.shape[-1]
    factor = 1.0 / (order * 4.0 * (modes * momenta) ** 0.5)
    row_groups = min(n, order // 16)
    col_groups = min(n // row_groups, order // 128)
    part_groups = n // (row_groups * col_groups)
    parts, rows, cols = 2 // part_groups, order // row_groups, order // col_groups
    sizes = (energies, momenta, modes, parts, rows, cols, row_groups, col_groups)
    vmem = pl.BlockSpec(memory_space=pltpu.VMEM)
    hbm = pl.BlockSpec(memory_space=pltpu.HBM)
    pieces = max(cols // 256, 1)
    exchanged = pltpu.VMEM((n, parts, rows, cols), jnp.bfloat16)
    block = pltpu.VMEM((2, order, order), jnp.bfloat16)
    wide = pltpu.VMEM((2, order, order), jnp.float32)
    return pl.pallas_call(
        functools.partial(kernel, sizes, factor),
        out_shape=tuple(jax.ShapeDtypeStruct(lesser.shape, jnp.bfloat16) for _ in range(3)),
        in_specs=[hbm] * 6,
        out_specs=(vmem, vmem, vmem),
        scratch_shapes=[
            pltpu.VMEM(retarded.shape, jnp.bfloat16),
            pltpu.SMEM(occupation.shape, jnp.float32),
            pltpu.SMEM(shift_slots.shape, jnp.int32),
            pltpu.SMEM(coupling.shape, jnp.int32),
            exchanged,
            exchanged,
            pltpu.VMEM((modes, energies + 1, momenta, parts, rows, cols), jnp.float32),
            exchanged,
            exchanged,
            block,
            block,
            block,
            block,
            wide,
            wide,
            wide,
            pltpu.SemaphoreType.DMA((3 + pieces,)),
            pltpu.SemaphoreType.DMA((3 + pieces,)),
            pltpu.SemaphoreType.DMA((1 + pieces,)),
            pltpu.SemaphoreType.DMA((4,)),
        ],
        compiler_params=pltpu.CompilerParams(
            collective_id=0, has_side_effects=True, vmem_limit_bytes=56 * 1024 * 1024
        ),
        cost_estimate=pl.CostEstimate(
            flops=48 * order**3, bytes_accessed=24 * order * order, transcendentals=0
        ),
    )(lesser, greater, retarded, occupation, shift_slots, coupling)


def solution(mesh):
    split = P("energy", "momentum", None, None, None)
    return jax.shard_map(
        functools.partial(per_device, mesh.shape["energy"], mesh.shape["momentum"]),
        mesh=mesh,
        in_specs=(split, split, split, P(), P(), P()),
        out_specs=(split, split, split),
        check_vma=False,
    )
```

```python
import functools

import jax
import jax.numpy as jnp
from jax import lax
from jax.experimental import pallas as pl
from jax.experimental.pallas import tpu as pltpu
from jax.sharding import PartitionSpec as P

MESH = pl.DeviceIdType.MESH


def dot(a, b):
    return jnp.dot(a, b, preferred_element_type=jnp.float32)


def dot_t(a, b):
    return lax.dot_general(a, b, (((1,), (1,)), ((), ())), preferred_element_type=jnp.float32)


def kernel(
    sizes,
    factor,
    less_ref,
    more_ref,
    ret_ref,
    occ_ref,
    shift_ref,
    coup_ref,
    less_out,
    more_out,
    ret_out,
    ret_held,
    occ_held,
    shift_held,
    coup_held,
    recv_less,
    recv_more,
    mixed,
    send_less,
    send_more,
    sig_less,
    sig_more,
    half,
    half_ret,
    half_less,
    sum_more,
    sum_ret,
    send_sem,
    recv_sem,
    own_sem,
    load_sem,
):
    energies, momenta, modes, parts, rows, cols, row_groups, col_groups = sizes
    n = energies * momenta
    my_e, my_m = lax.axis_index("energy"), lax.axis_index("momentum")
    me = my_e * momenta + my_m
    order = row_groups * rows

    pieces = max(cols // 256, 1)
    width = cols // pieces

    my_row = [lax.rem(my_m + m + 1, momenta) for m in range(momenta)]

    def others(act):
        def at_energy(t, carry):
            odd = lax.rem(t, 2)
            half_t = lax.div(t + odd, 2)
            offset = energies // 2 + half_t - 2 * odd * half_t
            e = lax.rem(my_e + offset, energies)
            for m in my_row:
                act(e, m)
            return carry

        lax.fori_loop(0, energies - 1, at_energy, 0)
        for m in my_row[:-1]:
            act(my_e, m)

    def piece(ref, lead, d, begin, count):
        row = pl.multiple_of(lax.rem(d, row_groups) * rows, rows)
        rest = lax.div(d, row_groups)
        col = pl.multiple_of(lax.rem(rest, col_groups) * cols, cols) + begin
        part = lax.div(rest, col_groups) * parts
        index = (pl.ds(part, parts), pl.ds(row, rows), pl.ds(col, count))
        return ref.at[(0,) * lead + index]

    barrier = pltpu.get_barrier_semaphore()

    def greet(e, m):
        pl.semaphore_signal(barrier, inc=1, device_id=(e, m), device_id_type=MESH)

    others(greet)
    loads = [
        pltpu.make_async_copy(piece(less_ref, 2, me, 0, cols), recv_less.at[me], own_sem.at[0]),
        pltpu.make_async_copy(piece(more_ref, 2, me, 0, cols), recv_more.at[me], own_sem.at[1]),
        pltpu.make_async_copy(ret_ref, ret_held, load_sem.at[0]),
        pltpu.make_async_copy(occ_ref, occ_held, load_sem.at[1]),
        pltpu.make_async_copy(shift_ref, shift_held, load_sem.at[2]),
        pltpu.make_async_copy(coup_ref, coup_held, load_sem.at[3]),
    ]
    for load in loads:
        load.start()
    pl.semaphore_wait(barrier, n - 1)

    def forward(ref, landing, which):
        def send(e, m):
            pltpu.make_async_remote_copy(
                src_ref=piece(ref, 2, e * momenta + m, 0, cols),
                dst_ref=landing.at[me],
                send_sem=send_sem.at[which],
                recv_sem=recv_sem.at[which],
                device_id=(e, m),
                device_id_type=MESH,
            ).start()

        others(send)

    def back(ref, landing, begin, count, which):
        def send(e, m):
            pltpu.make_async_remote_copy(
                src_ref=ref.at[e * momenta + m, :, :, pl.ds(begin, count)],
                dst_ref=piece(landing, 0, me, begin, count),
                send_sem=send_sem.at[which],
                recv_sem=recv_sem.at[which],
                device_id=(e, m),
                device_id_type=MESH,
            ).start()

        others(send)

    def wait_all(sem, count):
        span = recv_less.at[pl.ds(0, n - 1), :, :, pl.ds(0, count)]
        pltpu.make_async_copy(span, span, sem).wait()

    forward(less_ref, recv_less, 0)
    forward(more_ref, recv_more, 1)

    mixed[:, energies] = jnp.zeros((modes, momenta, parts, rows, cols), jnp.float32)

    def mix(recv, send, add_below, add_above, begin, count):
        step = min(count, 256)
        blocks = parts * (count // step)

        def place(i):
            b = lax.rem(i, blocks)
            col = begin + lax.rem(b, count // step) * step
            at = pl.ds(pl.multiple_of(col, step), step)
            return lax.div(i, blocks), lax.div(b, count // step), at

        def over_momenta(i, carry):
            s, part, at = place(i)
            terms = [recv[s * momenta + q, part, :, at].astype(jnp.float32) for q in range(momenta)]
            for m in range(modes):
                for k in range(momenta):
                    total = coup_held[m, k, 0].astype(jnp.float32) * terms[0]
                    for q in range(1, momenta):
                        total += coup_held[m, k, q].astype(jnp.float32) * terms[q]
                    mixed[m, s, k, part, :, at] = total
            return carry

        lax.fori_loop(0, energies * blocks, over_momenta, 0)

        def over_energies(i, carry):
            j, part, at = place(i)
            for k in range(momenta):
                total = None
                for m in range(modes):
                    phonons = occ_held[m]
                    for side, add in ((0, add_below), (1, add_above)):
                        term = ((phonons + add) * factor) * mixed[m, shift_held[m, side, j], k, part, :, at]
                        total = term if total is None else total + term
                send[j * momenta + k, part, :, at] = total.astype(jnp.bfloat16)
            return carry

        lax.fori_loop(0, energies * blocks, over_energies, 0)

    for load in loads[2:]:
        load.wait()
    loads[0].wait()
    wait_all(recv_sem.at[0], cols)
    mix(recv_less, send_less, 0.0, 1.0, 0, cols)
    back(send_less, sig_less, 0, cols, 2)
    keep_less = pltpu.make_async_copy(send_less.at[me], piece(sig_less, 0, me, 0, cols), own_sem.at[0])
    keep_less.start()

    loads[1].wait()
    wait_all(recv_sem.at[1], cols)
    keeps = []
    for c in range(pieces):
        begin = c * width
        mix(recv_more, send_more, 1.0, 0.0, begin, width)
        back(send_more, sig_more, begin, width, 3 + c)
        keep = pltpu.make_async_copy(
            send_more.at[me, :, :, pl.ds(begin, width)],
            piece(sig_more, 0, me, begin, width),
            own_sem.at[1 + c],
        )
        keep.start()
        keeps.append(keep)

    ret_re, ret_im = ret_held.at[0, 0, 0], ret_held.at[0, 0, 1]

    def halfway(sigma, at):
        re, im = sigma[0, :, at], sigma[1, :, at]
        left_re, left_im = ret_re[...], ret_im[...]
        return (
            dot(left_re, re) - dot(left_im, im),
            dot(left_re, im) + dot(left_im, re),
        )

    def adjoint(which, at, to):
        re, im = half[0, :, at], half[1, :, at]
        right_re, right_im = ret_re[to, at], ret_im[to, at]
        if which == 0:
            return dot_t(re, right_re) + dot_t(im, right_im)
        return dot_t(im, right_re) - dot_t(re, right_im)

    def dyson(which, at, to):
        re, im = half_ret[0, :, at], half_ret[1, :, at]
        right_re, right_im = ret_re[at, to], ret_im[at, to]
        if which == 0:
            return dot(re, right_re) - dot(im, right_im)
        return dot(re, right_im) + dot(im, right_re)

    tile = min(order, 256)
    tiles = [pl.ds(t * tile, tile) for t in range(order // tile)]

    keep_less.wait()
    wait_all(recv_sem.at[2], cols)
    for at in tiles:
        re, im = halfway(sig_less, at)
        half_less[0, :, at] = re
        half_less[1, :, at] = im
        half[0, :, at] = re.astype(jnp.bfloat16)
        half[1, :, at] = im.astype(jnp.bfloat16)
    for to in tiles:
        for x in range(2):
            less_out[0, 0, x, :, to] = adjoint(x, pl.ds(0, order), to).astype(jnp.bfloat16)

    stages = pieces if col_groups == 1 else 1
    span = order // stages
    for c in range(pieces):
        keeps[c].wait()
        wait_all(recv_sem.at[3 + c], width)
        if stages == 1 and c < pieces - 1:
            continue
        stage = c if stages > 1 else 0
        last = stage == stages - 1
        for t in range(span // tile):
            at = pl.ds(stage * span + t * tile, tile)
            for x, value in enumerate(halfway(sig_more, at)):
                half[x, :, at] = value.astype(jnp.bfloat16)
                half_ret[x, :, at] = ((value - half_less[x, :, at]) * 0.5).astype(jnp.bfloat16)
        at = pl.ds(stage * span, span)
        for to in tiles:
            for x in range(2):
                more, ret = adjoint(x, at, to), dyson(x, at, to)
                if stage > 0:
                    more += sum_more[x, :, to]
                    ret += sum_ret[x, :, to]
                if last:
                    more_out[0, 0, x, :, to] = more.astype(jnp.bfloat16)
                    ret += (ret_re, ret_im)[x][:, to].astype(jnp.float32)
                    ret_out[0, 0, x, :, to] = ret.astype(jnp.bfloat16)
                else:
                    sum_more[x, :, to] = more
                    sum_ret[x, :, to] = ret
    for which in range(3):
        wait_all(send_sem.at[which], cols)
    for c in range(pieces):
        wait_all(send_sem.at[3 + c], width)


def per_device(energies, momenta, lesser, greater, retarded, occupation, shift_slots, coupling):
    n = energies * momenta
    modes = coupling.shape[0]
    order = lesser.shape[-1]
    factor = 1.0 / (order * 4.0 * (modes * momenta) ** 0.5)
    row_groups = min(n, order // 16)
    col_groups = min(n // row_groups, order // 128)
    part_groups = n // (row_groups * col_groups)
    parts, rows, cols = 2 // part_groups, order // row_groups, order // col_groups
    sizes = (energies, momenta, modes, parts, rows, cols, row_groups, col_groups)
    vmem = pl.BlockSpec(memory_space=pltpu.VMEM)
    hbm = pl.BlockSpec(memory_space=pltpu.HBM)
    pieces = max(cols // 256, 1)
    exchanged = pltpu.VMEM((n, parts, rows, cols), jnp.bfloat16)
    block = pltpu.VMEM((2, order, order), jnp.bfloat16)
    wide = pltpu.VMEM((2, order, order), jnp.float32)
    return pl.pallas_call(
        functools.partial(kernel, sizes, factor),
        out_shape=tuple(jax.ShapeDtypeStruct(lesser.shape, jnp.bfloat16) for _ in range(3)),
        in_specs=[hbm] * 6,
        out_specs=(vmem, vmem, vmem),
        scratch_shapes=[
            pltpu.VMEM(retarded.shape, jnp.bfloat16),
            pltpu.SMEM(occupation.shape, jnp.float32),
            pltpu.SMEM(shift_slots.shape, jnp.int32),
            pltpu.SMEM(coupling.shape, jnp.int32),
            exchanged,
            exchanged,
            pltpu.VMEM((modes, energies + 1, momenta, parts, rows, cols), jnp.float32),
            exchanged,
            exchanged,
            block,
            block,
            block,
            block,
            wide,
            wide,
            wide,
            pltpu.SemaphoreType.DMA((3 + pieces,)),
            pltpu.SemaphoreType.DMA((3 + pieces,)),
            pltpu.SemaphoreType.DMA((1 + pieces,)),
            pltpu.SemaphoreType.DMA((4,)),
        ],
        compiler_params=pltpu.CompilerParams(
            collective_id=0, has_side_effects=True, vmem_limit_bytes=50 * 1024 * 1024
        ),
        cost_estimate=pl.CostEstimate(
            flops=48 * order**3, bytes_accessed=24 * order * order, transcendentals=0
        ),
    )(lesser, greater, retarded, occupation, shift_slots, coupling)


def solution(mesh):
    split = P("energy", "momentum", None, None, None)
    return jax.shard_map(
        functools.partial(per_device, mesh.shape["energy"], mesh.shape["momentum"]),
        mesh=mesh,
        in_specs=(split, split, split, P(), P(), P()),
        out_specs=(split, split, split),
        check_vma=False,
    )
```
